256 devices in a mesh: pop: 16 (over y, x), mp: 16 (over z, core).
Axes of the slice: x: 4, y: 4, z: 8, core: 2. Of those that a mesh axis runs over, the one named last changes fastest.
Arguments:
- tokens: bfloat16 [12288, 4096], P('pop', 'mp'), may hold values from -6 to 6
- weight: bfloat16 [4096, 16384], P('pop', 'mp'), may hold values from -6 to 6
- fitness: float32 [384], P('pop'), may hold values from 0.4 to 14.4
- row_factors: bfloat16 [384, 4096], P('pop'), may hold values from -6 to 6
- col_factors: bfloat16 [384, 16384], P('pop', 'mp'), may hold values from -6 to 6
Outputs:
- keys: bfloat16 [12288, 16384], P('pop', 'mp')
- new_weight: bfloat16 [4096, 16384], P('pop', 'mp')
The draws below stay inside these ranges and needn't reach their ends.
All inputs are finite; a program needn't handle non-finite values.
Results may differ from the reference program's by a relative error of at most 0.005.
Values may be sent and summed in bfloat16 or wider, within the bound.
A program may use at most 64 MiB of HBM per device.

```python
import math
import jax
import jax.numpy as jnp
from jax import lax

D = 4096
FF = 16384
TOK = 32
MEMBERS = 384


def draw_fitness(key, part):
    key = jax.random.fold_in(key, 7)
    index = jnp.arange(MEMBERS, dtype=jnp.float32)
    rising = 1.0 + 2.0 * index / (MEMBERS - 1)
    noise = jax.random.uniform(key, (MEMBERS,), jnp.float32, -1.0, 1.0)
    return (rising * (1.0 + 0.6 * noise)).astype(jnp.float32)


def steps_of(key, extent, split, smallest, top_value):
    level = 1.0
    for dim, parts in split:
        draws = jax.random.uniform(jax.random.fold_in(jax.random.fold_in(key, 6), dim), (parts,), jnp.float32, smallest / len(split), top_value / len(split))
        level = level * jnp.repeat(jnp.exp(draws), extent[dim] // parts).reshape((-1,) + (1,) * (len(extent) - 1 - dim))
    return level


def centred(rng, shape, spread, most, split=(), kind=jnp.bfloat16):
    result = spread * jax.random.normal(rng, shape, jnp.float32)
    if split:
        result = result * steps_of(rng, shape, split, -0.22, 0.18)
    return jnp.clip(result, -most, most).astype(kind)


def setup_inputs(seed: int = 0) -> dict:
    arg_keys = jax.random.split(jax.random.key(seed), 6)
    return {
        "tokens": centred(arg_keys[0], (MEMBERS * TOK, D), 1.0, 6.0, ((0, 16), (1, 16))),
        "weight": centred(arg_keys[1], (D, FF), 1.0, 6.0, ((0, 16), (1, 16))),
        "fitness": draw_fitness(jax.random.fold_in(arg_keys[5], 71), 0),
        "row_factors": centred(arg_keys[3], (MEMBERS, D), 1.0, 6.0, ((0, 16),)),
        "col_factors": centred(arg_keys[4], (MEMBERS, FF), 1.0, 6.0, ((0, 16), (1, 16))),
    }


def reference(tokens, weight, fitness, row_factors, col_factors):
    members = fitness.shape[0]
    grouped = tokens.reshape(members, TOK, D)

    def one_member(items):
        rows, arow, brow = items
        base = jnp.dot(rows, weight, preferred_element_type=jnp.float32)
        proj = jnp.dot(rows, arow, preferred_element_type=jnp.float32)
        h = (base + 0.3 * proj[:, None] * brow.astype(jnp.float32)[None, :]) / math.sqrt(D)
        return (jnp.maximum(h, 0.0) ** 2).astype(jnp.bfloat16)
    keys = lax.map(one_member, (grouped, row_factors, col_factors)).reshape(members * TOK, FF)
    mean = jnp.sum(fitness) / members
    var = jnp.sum(fitness * fitness) / members - mean * mean
    shaped = (fitness - mean) / jnp.sqrt(var + 1e-05)
    scaled = (shaped[:, None] * col_factors.astype(jnp.float32) / math.sqrt(members)).astype(jnp.bfloat16)
    delta = jnp.dot(row_factors.T, scaled, preferred_element_type=jnp.float32)
    new_weight = (weight.astype(jnp.float32) + 0.5 * delta).astype(jnp.bfloat16)
    return (keys, new_weight)
```

```python
import math

import jax
import jax.numpy as jnp
from jax import lax
from jax.experimental import pallas as pl
from jax.experimental.pallas import tpu as pltpu
from jax.sharding import PartitionSpec as P

D = 4096
N = 4
NZ = 8
POP = N * N
MEMB = 24
TOK = 32
ROWS = MEMB * TOK
FEAT = 256
HID = 1024
HALF = HID // 2
COUNT = POP * MEMB
MESH = pl.DeviceIdType.MESH

ORDER = (
    ("C", 1, 0, 0), ("C", 3, 0, 0), ("C", 0, 1, 0), ("C", 0, 3, 0),
    ("W", 1, 0, 0), ("W", 3, 0, 1), ("W", 0, 1, 0), ("W", 0, 3, 1),
    ("T", 1),
    ("C", 2, 0, 0), ("C", 2, 0, 1),
    ("W", 1, 0, 1), ("W", 3, 0, 0), ("W", 0, 1, 1), ("W", 0, 3, 0),
    ("C", 1, 1, 0), ("C", 1, 3, 0), ("C", 3, 1, 0), ("C", 3, 3, 0),
    ("C", 0, 2, 0), ("C", 0, 2, 1),
    ("T", 2),
    ("W", 2, 0, 1), ("W", 2, 0, 0), ("W", 1, 1, 0), ("W", 1, 3, 0),
    ("W", 3, 1, 1), ("W", 3, 3, 1), ("W", 0, 2, 0), ("W", 0, 2, 1),
    ("T", 3),
    ("W", 1, 1, 1), ("W", 1, 3, 1), ("W", 3, 1, 0), ("W", 3, 3, 0),
    ("C", 2, 1, 0), ("C", 2, 3, 0), ("C", 1, 2, 0), ("C", 1, 2, 1),
    ("C", 3, 2, 0), ("C", 3, 2, 1),
    ("T", 4),
    ("G", ((0, 0), (0, 1), (0, 3), (0, 2))),
    ("W", 2, 3, 1), ("W", 2, 1, 1),
    ("G", ((1, 0), (1, 1), (1, 3))),
    ("W", 2, 3, 0), ("W", 2, 1, 0),
    ("G", ((3, 0), (3, 1), (3, 3))),
    ("W", 3, 2, 1), ("W", 1, 2, 0),
    ("G", ((2, 0), (2, 1), (2, 3))),
    ("W", 1, 2, 1), ("W", 3, 2, 0),
    ("G", ((1, 2), (3, 2))),
    ("C", 2, 2, 0), ("C", 2, 2, 1),
    ("D",),
)


def kernel(tok, w, fit, row, col, keys, neww,
           wbuf, tbuf, cbuf, rbuf, rsrc, fbuf, fsrc, csrc, rowf, colf, shp, scaled, rfull,
           acc, pacc, kst, nst, ssem, rsem, lsem):
    p, m = lax.axis_index("pop"), lax.axis_index("mp")
    x, y, z, c = lax.rem(p, N), lax.div(p, N), lax.div(m, 2), lax.rem(m, 2)
    a, b = x * (1 - c) + y * c, y * (1 - c) + x * c

    def group(ga, gb):
        ga, gb = lax.rem(ga, N), lax.rem(gb, N)
        return (gb * (1 - c) + ga * c) * N + ga * (1 - c) + gb * c

    def plane(dz, dc=0):
        return lax.rem(z + dz + NZ, NZ) * 2 + lax.rem(c + dc, 2)

    src = {(i, j): group(a + N - i, b + N - j) for i in range(N) for j in range(N)}
    links = {
        "a+": (group(a + 1, b), m), "a-": (group(a + 3, b), m),
        "b+": (group(a, b + 1), m), "b-": (group(a, b + 3), m),
        "z+": (p, plane(1)), "z-": (p, plane(-1)), "s": (p, plane(0, 1)),
    }
    far = [(i, j) for i in range(N) for j in range(N) if (i, j) != (0, 0)]

    barrier = pltpu.get_barrier_semaphore()
    partners = [(src[ij], m) for ij in far] + [links["z+"], links["z-"], links["s"]]
    for dev in partners:
        pl.semaphore_signal(barrier, inc=1, device_id=dev, device_id_type=MESH)

    colv = col[...].astype(jnp.float32)
    colf[0] = colv[:, :HALF]
    colf[1] = colv[:, HALF:]
    own_col = jnp.concatenate([colv[:, :HALF], colv[:, HALF:]], axis=0).astype(jnp.bfloat16)
    csrc[...] = own_col
    cbuf[p] = own_col
    for q in range(POP):
        piece = row[:, q * FEAT:(q + 1) * FEAT].astype(jnp.float32)
        rowf[q] = piece
        rsrc[q] = jnp.concatenate([piece[:, :128], piece[:, 128:]], axis=0).astype(jnp.bfloat16)
    sub = lax.broadcasted_iota(jnp.int32, (8, 128), 0)
    lane = lax.broadcasted_iota(jnp.int32, (8, 128), 1)
    tile = jnp.zeros((8, 128), jnp.float32)
    for i in range(MEMB):
        tile = jnp.where((sub == i % 8) & (lane == i // 8), fit[i], tile)
    fsrc[...] = tile
    fbuf[p] = tile

    pl.semaphore_wait(barrier, len(partners))

    copies = {}

    def send(key, source, target, dev):
        n = len(copies)
        copy = pltpu.make_async_remote_copy(
            src_ref=source, dst_ref=target, send_sem=ssem.at[n], recv_sem=rsem.at[n],
            device_id=dev, device_id_type=MESH,
        )
        copy.start()
        copies[key] = copy

    def send_w(link, key, half, source=None):
        slot = src[back(key, link)]
        source = wbuf.at[slot, half] if source is None else source
        send(("W", *key, half), source, wbuf.at[slot, half], links[link])

    def back(key, link):
        i, j = key
        step = {"a+": (1, 0), "a-": (3, 0), "b+": (0, 1), "b-": (0, 3)}[link]
        return ((i - step[0]) % N, (j - step[1]) % N)

    def send_c(link, key, part, lo=0, rows=2 * MEMB):
        slot = src[back(key, link)]
        source = csrc if back(key, link) == (0, 0) else cbuf.at[slot]
        send(("C", *key, part), source.at[pl.ds(lo, rows)], cbuf.at[slot, pl.ds(lo, rows)], links[link])

    def own_w(half):
        return w.at[:, pl.ds(half * HALF, HALF)]

    send_c("a+", (1, 0), 0)
    send_c("a-", (3, 0), 0)
    send_w("a+", (1, 0), 0, own_w(0))
    send_w("a-", (3, 0), 1, own_w(1))
    send_c("b+", (0, 1), 0)
    send_c("b-", (0, 3), 0)
    send_w("b+", (0, 1), 0, own_w(0))
    send_w("b-", (0, 3), 1, own_w(1))
    for dz, link in ((1, "z+"), (-1, "z-")):
        send(("T", dz), tok, tbuf.at[m], links[link])
    send_w("a+", (1, 0), 1, own_w(1))
    send_w("a-", (3, 0), 0, own_w(0))
    send_w("b+", (0, 1), 1, own_w(1))
    send_w("b-", (0, 3), 0, own_w(0))
    send(("S", 0), tok, tbuf.at[m], links["s"])
    for i, j in far:
        to = group(a + i, b + j)
        send(("R", i, j), rsrc.at[to], rbuf.at[p], (to, m))
        send(("F", i, j), fsrc, fbuf.at[p], (to, m))

    local = [
        pltpu.make_async_copy(tok, tbuf.at[m], lsem.at[0]),
        pltpu.make_async_copy(own_w(0), wbuf.at[p, 0], lsem.at[1]),
        pltpu.make_async_copy(own_w(1), wbuf.at[p, 1], lsem.at[2]),
        pltpu.make_async_copy(rsrc.at[p], rbuf.at[p], lsem.at[3]),
    ]
    for copy in local:
        copy.start()
    pacc[...] = jnp.zeros_like(pacc)
    for copy in local:
        copy.wait()

    def project(blocks):
        @pl.loop(0, MEMB)
        def _(k):
            rows = pl.ds(pl.multiple_of(k * TOK, TOK), TOK)
            total = pacc[rows, :]
            for f in blocks:
                term = tbuf[f, rows, :].astype(jnp.float32) * rowf[f, pl.ds(k, 1), :]
                total = total + (term[:, :128] + term[:, 128:])
            pacc[rows, :] = total

    def take_t(d):
        if d < 4:
            for dz in (d, -d):
                copies["T", dz].wait_recv()
                way = 1 if dz > 0 else -1
                f = plane(-dz)
                if d < 3:
                    send(("T", dz + way), tbuf.at[f], tbuf.at[f], links["z+" if way > 0 else "z-"])
                else:
                    part = pl.ds(0 if way > 0 else ROWS // 2, ROWS // 2)
                    send(("T", 4 * way), tbuf.at[f, part], tbuf.at[f, part], links["z+" if way > 0 else "z-"])
                send(("S", dz), tbuf.at[f], tbuf.at[f], links["s"])
            near = (d - 1, 1 - d) if d > 1 else (0,)
        else:
            f = plane(4)
            for dz in (4, -4):
                copies["T", dz].wait_recv()
                part = pl.ds(0 if dz > 0 else ROWS // 2, ROWS // 2)
                send(("S", dz), tbuf.at[f, part], tbuf.at[f, part], links["s"])
            near = (3, -3)
        for dz in near:
            copies["S", dz].wait_recv()
        project([plane(-dz, dc) for dz in near for dc in (0, 1)])
        if d == 4:
            for dz in (4, -4):
                copies["S", dz].wait_recv()
            project([plane(4), plane(4, 1)])

            @pl.loop(0, MEMB)
            def _(k):
                rows = pl.ds(pl.multiple_of(k * TOK, TOK), TOK)
                proj = 0.3 * jnp.sum(pacc[rows, :], axis=1, keepdims=True)
                for s in range(2):
                    acc[s, rows, :] = proj * colf[s, pl.ds(k, 1), :]

    def take_w(i, j, s):
        copies["W", i, j, s].wait_recv()
        if j == 0:
            if (i, s) == (1, 0):
                send_w("a+", (2, 0), 0)
            if (i, s) == (3, 1):
                send_w("a-", (2, 0), 1)
            send_w("b+", (i, 1), s)
            send_w("b-", (i, 3), s)
        elif (j, s) == (1, 0):
            send_w("b+", (i, 2), 0)
        elif (j, s) == (3, 1):
            send_w("b-", (i, 2), 1)

    def take_c(i, j, part):
        copies["C", i, j, part].wait_recv()
        if j == 0:
            if i == 1:
                send_c("a+", (2, 0), 0, 0, 32)
            if i == 3:
                send_c("a-", (2, 0), 1, 32, 16)
            if i != 2 or part == 1:
                send_c("b+", (i, 1), 0)
                send_c("b-", (i, 3), 0)
        elif j == 1:
            send_c("b+", (i, 2), 0, 0, 16 if i in (0, 2) else 32)
        elif j == 3:
            lo = 16 if i in (0, 2) else 32
            send_c("b-", (i, 2), 1, lo, 48 - lo)

    def multiply(s, rows, blocks):
        total = None
        for ij in blocks:
            f = src[ij]
            part = jnp.dot(tbuf[f, rows, :], wbuf[f, s], preferred_element_type=jnp.float32)
            total = part if total is None else total + part
        return total

    def gather(blocks):
        @pl.loop(0, 6)
        def _(t):
            s, r = lax.div(t, 3), lax.rem(t, 3)
            rows = pl.ds(pl.multiple_of(r * 256, 256), 256)
            acc[s, rows, :] += multiply(s, rows, blocks)

    def delta():
        for ij in far:
            copies["R", *ij].wait_recv()
            copies["F", *ij].wait_recv()
        fb = fbuf[...]
        lanes = lax.broadcasted_iota(jnp.int32, fb.shape, 2)
        cols = [jnp.sum(jnp.where(lanes == q, fb, 0.0), axis=2, keepdims=True) for q in range(3)]
        total = sum(jnp.sum(v) for v in cols)
        square = sum(jnp.sum(v * v) for v in cols)
        mean = total / COUNT
        var = square / COUNT - mean * mean
        scale = jnp.sqrt(jnp.full((1, 1, 1), var + 1e-05, jnp.float32))
        for q in range(3):
            shp[:, q * 8:(q + 1) * 8, :] = jnp.broadcast_to((cols[q] - mean) / scale, (POP, 8, 128))

        @pl.loop(0, POP // 2)
        def _(t):
            out = pl.ds(pl.multiple_of(t * 48, 48), 48)
            two = (2 * t, 2 * t + 1)
            for h in range(2):
                part = slice(h * MEMB, (h + 1) * MEMB)
                scaled[h, out, :] = jnp.concatenate(
                    [shp[q][:, 0:1] * cbuf[q].astype(jnp.float32)[part] / math.sqrt(COUNT) for q in two], axis=0
                ).astype(jnp.bfloat16)
                rfull[out, h * 128:(h + 1) * 128] = jnp.concatenate(
                    [rbuf[q].astype(jnp.float32)[part] for q in two], axis=0
                )
        left = jnp.transpose(rfull[...]).astype(jnp.bfloat16)
        for h in range(2):
            part = slice(h * HALF, (h + 1) * HALF)
            d = jnp.dot(left, scaled[h], preferred_element_type=jnp.float32)
            nst[:, part] = (w[:, part].astype(jnp.float32) + 0.5 * d).astype(jnp.bfloat16)
        copy = pltpu.make_async_copy(nst, neww, lsem.at[4])
        copy.start()
        return copy

    outs = []
    for step in ORDER:
        if step[0] == "W":
            take_w(*step[1:])
        elif step[0] == "C":
            take_c(*step[1:])
        elif step[0] == "T":
            take_t(*step[1:])
        elif step[0] == "G":
            gather(step[1])
        else:
            outs.append(delta())

    for n, s in enumerate((1, 0)):
        copies["W", 2, 2, s].wait_recv()
        for r in range(3):
            rows = pl.ds(r * 256, 256)
            h = (acc[s, rows, :] + multiply(s, rows, [(2, 2)])) / math.sqrt(D)
            kst[s, rows, :] = (jnp.maximum(h, 0.0) ** 2).astype(jnp.bfloat16)
            copy = pltpu.make_async_copy(
                kst.at[s, rows], keys.at[rows, pl.ds(s * HALF, HALF)], lsem.at[5 + n * 3 + r]
            )
            copy.start()
            outs.append(copy)
    for copy in outs:
        copy.wait()
    for copy in copies.values():
        copy.wait_send()


def local(tokens, weight, fitness, row_factors, col_factors):
    vmem = pl.BlockSpec(memory_space=pltpu.VMEM)
    hbm = pl.BlockSpec(memory_space=pl.ANY)
    bf, f32 = jnp.bfloat16, jnp.float32
    return pl.pallas_call(
        kernel,
        out_shape=(
            jax.ShapeDtypeStruct((ROWS, HID), bf),
            jax.ShapeDtypeStruct((FEAT, HID), bf),
        ),
        in_specs=[vmem, vmem, pl.BlockSpec(memory_space=pltpu.SMEM), vmem, vmem],
        out_specs=(hbm, hbm),
        scratch_shapes=[
            pltpu.VMEM((POP, 2, FEAT, HALF), bf),
            pltpu.VMEM((2 * NZ, ROWS, FEAT), bf),
            pltpu.VMEM((POP, 2 * MEMB, HALF), bf),
            pltpu.VMEM((POP, 2 * MEMB, 128), bf),
            pltpu.VMEM((POP, 2 * MEMB, 128), bf),
            pltpu.VMEM((POP, 8, 128), f32),
            pltpu.VMEM((8, 128), f32),
            pltpu.VMEM((2 * MEMB, HALF), bf),
            pltpu.VMEM((POP, MEMB, FEAT), f32),
            pltpu.VMEM((2, MEMB, HALF), f32),
            pltpu.VMEM((POP, MEMB, 128), f32),
            pltpu.VMEM((2, COUNT, HALF), bf),
            pltpu.VMEM((COUNT, FEAT), f32),
            pltpu.VMEM((2, ROWS, HALF), f32),
            pltpu.VMEM((ROWS, 128), f32),
            pltpu.VMEM((2, ROWS, HALF), bf),
            pltpu.VMEM((FEAT, HID), bf),
            pltpu.SemaphoreType.DMA((128,)),
            pltpu.SemaphoreType.DMA((128,)),
            pltpu.SemaphoreType.DMA((16,)),
        ],
        compiler_params=pltpu.CompilerParams(
            collective_id=0, has_side_effects=True, vmem_limit_bytes=48 << 20
        ),
        cost_estimate=pl.CostEstimate(flops=6_700_000_000, bytes_accessed=4_000_000, transcendentals=0),
    )(tokens, weight, fitness, row_factors, col_factors)


def solution(mesh):
    placed = (P("pop", "mp"), P("pop", "mp"), P("pop"), P("pop", None), P("pop", "mp"))
    return jax.shard_map(
        local,
        mesh=mesh,
        in_specs=placed,
        out_specs=(P("pop", "mp"), P("pop", "mp")),
        check_vma=False,
    )
```

```python
import math

import jax
import jax.numpy as jnp
from jax import lax
from jax.experimental import pallas as pl
from jax.experimental.pallas import tpu as pltpu
from jax.sharding import PartitionSpec as P

D = 4096
N = 4
NZ = 8
POP = N * N
MEMB = 24
TOK = 32
ROWS = MEMB * TOK
FEAT = 256
HID = 1024
HALF = HID // 2
COUNT = POP * MEMB
MESH = pl.DeviceIdType.MESH

ORDER = (
    ("C", 1, 0, 0), ("C", 3, 0, 0), ("C", 0, 1, 0), ("C", 0, 3, 0),
    ("I",), ("Z",), ("R",),
    ("W", 1, 0, 0), ("W", 3, 0, 1), ("W", 0, 1, 0), ("W", 0, 3, 1),
    ("C", 2, 0, 0), ("C", 2, 0, 1), ("C", 1, 1, 0), ("C", 1, 3, 0),
    ("C", 3, 1, 0), ("C", 3, 3, 0), ("C", 0, 2, 0), ("C", 0, 2, 1),
    ("W", 3, 0, 0), ("W", 1, 0, 1),
    ("T", 1),
    ("W", 0, 1, 1), ("W", 0, 3, 0), ("W", 2, 0, 1), ("W", 2, 0, 0),
    ("W", 1, 1, 0), ("W", 1, 3, 0),
    ("T", 2),
    ("W", 3, 1, 1), ("W", 3, 3, 1), ("S", (2, -2)), ("A", 0), ("A", 4), ("W", 0, 2, 0), ("W", 0, 2, 1), ("A", 8), ("A", 12),
    ("C", 2, 1, 0), ("C", 2, 3, 0), ("C", 1, 2, 1), ("C", 1, 2, 0),
    ("C", 3, 2, 1), ("C", 3, 2, 0),
    ("W", 3, 3, 0), ("W", 3, 1, 0),
    ("T", 3),
    ("W", 1, 3, 1), ("W", 1, 1, 1),
    ("S", (3, -3)),
    ("E", 0), ("E", 4),
    ("W", 2, 3, 1), ("W", 2, 1, 1),
    ("E", 8), ("E", 12),
    ("T", 4),
    ("W", 2, 3, 0), ("W", 2, 1, 0),
    ("K",),
    ("W", 3, 2, 1), ("W", 1, 2, 0),
    ("G", 2, 1), ("G", 2, 3),
    ("C", 2, 2, 1), ("C", 2, 2, 0),
    ("W", 1, 2, 1), ("W", 3, 2, 0),
    ("D",),
    ("G", 1, 2), ("G", 3, 2),
)


def kernel(tok, w, fit, row_in, col_in, keys, neww,
           row, col, wbuf, tbuf, cbuf, rbuf, rsrc, csrc, rowf, colf, shp, scaled, rfull,
           acc, pacc, ssem, rsem, lsem, ready):
    p, m = lax.axis_index("pop"), lax.axis_index("mp")
    x, y, z, c = lax.rem(p, N), lax.div(p, N), lax.div(m, 2), lax.rem(m, 2)
    a, b = x * (1 - c) + y * c, y * (1 - c) + x * c

    def group(ga, gb):
        ga, gb = lax.rem(ga, N), lax.rem(gb, N)
        return (gb * (1 - c) + ga * c) * N + ga * (1 - c) + gb * c

    def plane(dz, dc=0):
        return lax.rem(z + dz + NZ, NZ) * 2 + lax.rem(c + dc, 2)

    src = {(i, j): group(a + N - i, b + N - j) for i in range(N) for j in range(N)}
    links = {
        "a+": (group(a + 1, b), m), "a-": (group(a + 3, b), m),
        "b+": (group(a, b + 1), m), "b-": (group(a, b + 3), m),
        "z+": (p, plane(1)), "z-": (p, plane(-1)), "s": (p, plane(0, 1)),
    }
    far = [(i, j) for i in range(N) for j in range(N) if (i, j) != (0, 0)]

    def own_w(half):
        return w.at[:, pl.ds(half * HALF, HALF)]

    loads = [
        pltpu.make_async_copy(col_in, col, lsem.at[0]),
        pltpu.make_async_copy(row_in, row, lsem.at[1]),
        pltpu.make_async_copy(own_w(0), wbuf.at[p, 0], lsem.at[2]),
        pltpu.make_async_copy(own_w(1), wbuf.at[p, 1], lsem.at[3]),
        pltpu.make_async_copy(tok, tbuf.at[m], lsem.at[4]),
    ]
    for copy in loads:
        copy.start()

    barrier = pltpu.get_barrier_semaphore()

    def signal(sem, dev):
        pl.semaphore_signal(sem, inc=1, device_id=dev, device_id_type=MESH)

    signal(barrier, links["s"])
    for link in ("a+", "a-", "b+", "b-"):
        signal(barrier, (links[link][0], 2 * z))
    for q in range(2):
        @pl.when(p != 2 * z + q)
        def _(q=q):
            signal(barrier, (2 * z + q, 2 * z))
    for dz in (1, -1):
        signal(barrier, (p, lax.rem(z + dz + NZ, NZ) * 2 + 1))
    source = jnp.where(lax.div(p, 2) == z, 1, 0)

    loads[0].wait()
    colv = col[...].astype(jnp.float32)
    colf[0] = colv[:, :HALF]
    colf[1] = colv[:, HALF:]
    own_col = jnp.concatenate([colv[:, :HALF], colv[:, HALF:]], axis=0).astype(jnp.bfloat16)
    csrc[...] = own_col
    cbuf[p] = own_col

    @pl.when(c == 0)
    def _():
        pl.semaphore_wait(barrier, 9 + 30 * source)
        signal(ready.at[0], links["s"])

    @pl.when(c == 1)
    def _():
        pl.semaphore_wait(ready.at[0], 1)

    copies = {}

    def send(key, source, target, dev):
        n = len(copies)
        copy = pltpu.make_async_remote_copy(
            src_ref=source, dst_ref=target, send_sem=ssem.at[n], recv_sem=rsem.at[n],
            device_id=dev, device_id_type=MESH,
        )
        copy.start()
        copies[key] = copy

    def send_w(link, key, half, source=None):
        slot = src[back(key, link)]
        source = wbuf.at[slot, half] if source is None else source
        send(("W", *key, half), source, wbuf.at[slot, half], links[link])

    def back(key, link):
        i, j = key
        step = {"a+": (1, 0), "a-": (3, 0), "b+": (0, 1), "b-": (0, 3)}[link]
        return ((i - step[0]) % N, (j - step[1]) % N)

    def send_c(link, key, part, lo=0, rows=2 * MEMB):
        slot = src[back(key, link)]
        source = csrc if back(key, link) == (0, 0) else cbuf.at[slot]
        send(("C", *key, part), source.at[pl.ds(lo, rows)], cbuf.at[slot, pl.ds(lo, rows)], links[link])

    send_c("a+", (1, 0), 0)
    send_c("a-", (3, 0), 0)
    send_c("b+", (0, 1), 0)
    send_c("b-", (0, 3), 0)
    send_w("a+", (1, 0), 0, own_w(0))
    send_w("a-", (3, 0), 1, own_w(1))
    send_w("b+", (0, 1), 0, own_w(0))
    send_w("b-", (0, 3), 1, own_w(1))
    send(("S", 0), tok, tbuf.at[m], links["s"])

    loads[1].wait()
    for q in range(POP):
        rowf[q] = row[:, q * FEAT:(q + 1) * FEAT].astype(jnp.float32)

    def pieces(some=far):
        return [
            pltpu.make_async_remote_copy(
                src_ref=rsrc.at[group(a + i, b + j)], dst_ref=rbuf.at[m],
                send_sem=ssem.at[120 + n], recv_sem=rsem.at[120],
                device_id=(group(a + i, b + j), m), device_id_type=MESH,
            )
            for n, (i, j) in enumerate(some)
        ]

    @pl.when(p == m)
    def _():
        lane = lax.broadcasted_iota(jnp.int32, (8, FEAT), 1)
        sub = lax.broadcasted_iota(jnp.int32, (8, FEAT), 0)
        value = jnp.zeros((8, FEAT), jnp.float32)
        for i in range(MEMB):
            value = jnp.where(lane == i, fit[i], value)
        high = value.astype(jnp.bfloat16).astype(jnp.float32)
        middle = (value - high).astype(jnp.bfloat16).astype(jnp.float32)
        low = value - high - middle
        tile = jnp.where(sub == 0, high, jnp.where(sub == 1, middle, jnp.where(sub == 2, low, 0.0)))
        for q in range(POP):
            rsrc[q] = jnp.concatenate([rowf[q], tile], axis=0).astype(jnp.bfloat16)
        for copy in pieces():
            copy.start()
        rbuf[m] = rsrc[p]

    pacc[...] = jnp.zeros_like(pacc)
    acc[...] = jnp.zeros_like(acc)
    for copy in loads[2:]:
        copy.wait()

    def project(blocks):
        if not blocks:
            return

        @pl.loop(0, MEMB)
        def _(k):
            rows = pl.ds(pl.multiple_of(k * TOK, TOK), TOK)
            total = pacc[rows, :]
            for f in blocks:
                term = tbuf[f, rows, :].astype(jnp.float32) * rowf[f, pl.ds(k, 1), :]
                total = total + (term[:, :128] + term[:, 128:])
            pacc[rows, :] = total

    def take_s(steps):
        for dz in steps:
            copies["S", dz].wait_recv()
        project([plane(-dz, dc) for dz in steps for dc in (0, 1)])

    def take_t(d):
        if d < 4:
            for dz in (d, -d):
                copies["T", dz].wait_recv()
                way = 1 if dz > 0 else -1
                f = plane(-dz)
                if d < 3:
                    send(("T", dz + way), tbuf.at[f], tbuf.at[f], links["z+" if way > 0 else "z-"])
                    copies["R", dz].wait_recv()
                    send(("R", dz + way), rbuf.at[f], rbuf.at[f], links["z+" if way > 0 else "z-"])
                else:
                    part = pl.ds(0 if way > 0 else ROWS // 2, ROWS // 2)
                    send(("T", 4 * way), tbuf.at[f, part], tbuf.at[f, part], links["z+" if way > 0 else "z-"])
                    copies["R", dz].wait_recv()
                    if way > 0:
                        send(("R", 4), rbuf.at[f], rbuf.at[f], links["z+"])
                send(("S", dz), tbuf.at[f], tbuf.at[f], links["s"])
                send(("Q", dz), rbuf.at[f], rbuf.at[f], links["s"])
            near = {1: (0,), 2: (1, -1), 3: ()}[d]
        else:
            f = plane(4)
            for dz in (4, -4):
                copies["T", dz].wait_recv()
                part = pl.ds(0 if dz > 0 else ROWS // 2, ROWS // 2)
                send(("S", dz), tbuf.at[f, part], tbuf.at[f, part], links["s"])
            copies["R", 4].wait_recv()
            send(("Q", 4), rbuf.at[f], rbuf.at[f], links["s"])
            near = ()
        take_s(near)
        if d == 4:
            for dz in (4, -4):
                copies["S", dz].wait_recv()
            project([plane(4), plane(4, 1)])

            @pl.loop(0, MEMB)
            def _(k):
                rows = pl.ds(pl.multiple_of(k * TOK, TOK), TOK)
                proj = 0.3 * jnp.sum(pacc[rows, :], axis=1, keepdims=True)
                for s in range(2):
                    acc[s, rows, :] += proj * colf[s, pl.ds(k, 1), :]

    def take_w(i, j, s):
        copies["W", i, j, s].wait_recv()
        if j == 0:
            if (i, s) == (1, 0):
                send_w("a+", (2, 0), 0)
            if (i, s) == (3, 1):
                send_w("a-", (2, 0), 1)
            send_w("b+", (i, 1), s)
            send_w("b-", (i, 3), s)
        elif (j, s) == (1, 0):
            send_w("b+", (i, 2), 0)
        elif (j, s) == (3, 1):
            send_w("b-", (i, 2), 1)

    def take_c(i, j, part):
        copies["C", i, j, part].wait_recv()
        if j == 0:
            if i == 1:
                send_c("a+", (2, 0), 0, 0, 32)
            if i == 3:
                send_c("a-", (2, 0), 1, 32, 16)
            if i != 2 or part == 1:
                send_c("b+", (i, 1), 0)
                send_c("b-", (i, 3), 0)
        elif j == 1:
            send_c("b+", (i, 2), 0, 0, 16 if i in (0, 2) else 32)
        elif j == 3:
            lo = 16 if i in (0, 2) else 32
            send_c("b-", (i, 2), 1, lo, 48 - lo)

    def gather(f):
        for s in range(2):
            acc[s] += jnp.dot(tbuf[f], wbuf[f, s], preferred_element_type=jnp.float32)

    def place(f):
        fx, fy = lax.rem(f, N), lax.div(f, N)
        i = lax.rem(a + N - (fx * (1 - c) + fy * c), N)
        j = lax.rem(b + N - (fy * (1 - c) + fx * c), N)
        dz = lax.rem(lax.div(f, 2) + NZ - z, NZ)
        return i, j, jnp.minimum(dz, NZ - dz)

    def early(f):
        i, j, _ = place(f)
        return (i == 0) | (j == 0) | ((i != 2) & (j != 2))

    def first(f):
        i, j, d = place(f)
        return (((i == 0) & (j != 2)) | (j == 0)) & (d <= 2)

    def gather_first(start):
        @pl.loop(start, start + 4)
        def _(f):
            @pl.when(first(f))
            def _():
                gather(f)

    def gather_near(start):
        @pl.loop(start, start + 4)
        def _(f):
            @pl.when(early(f) & jnp.logical_not(first(f)) & (place(f)[2] <= 3))
            def _():
                gather(f)

    def gather_far():
        for dc in range(2):
            f = plane(4, dc)

            @pl.when(early(f))
            def _(f=f):
                gather(f)

    def start_z():
        @pl.when(c == 1)
        def _():
            pl.semaphore_wait(barrier, 5)
            signal(ready.at[1], links["s"])

        @pl.when(c == 0)
        def _():
            pl.semaphore_wait(ready.at[1], 1)

        for dz, link in ((1, "z+"), (-1, "z-")):
            send(("T", dz), tok, tbuf.at[m], links[link])

    def start_r():
        @pl.when(p != m)
        def _():
            pieces(far[:1])[0].wait_recv()

        for dz, link in ((1, "z+"), (-1, "z-")):
            send(("R", dz), rbuf.at[m], rbuf.at[m], links[link])
        send(("Q", 0), rbuf.at[m], rbuf.at[m], links["s"])

    def rest_of_own():
        send_w("a+", (1, 0), 1, own_w(1))
        send_w("a-", (3, 0), 0, own_w(0))
        send_w("b+", (0, 1), 1, own_w(1))
        send_w("b-", (0, 3), 0, own_w(0))

    def delta():
        for dz in (0, 1, -1, 2, -2, 3, -3, 4):
            copies["Q", dz].wait_recv()
        diagonal = lax.broadcasted_iota(jnp.int32, (MEMB, 128), 0) == lax.broadcasted_iota(jnp.int32, (MEMB, 128), 1)
        sums = jnp.zeros((1, 128), jnp.float32)
        squares = jnp.zeros((1, 128), jnp.float32)
        for q in range(POP):
            piece = rbuf[q].astype(jnp.float32)
            rfull[q * MEMB:(q + 1) * MEMB, :] = piece[:MEMB]
            tail = piece[MEMB:, :128]
            value = (tail[0:1] + tail[1:2]) + tail[2:3]
            sums += value
            squares += value * value
            column = jnp.sum(jnp.where(diagonal, value, 0.0), axis=1, keepdims=True)
            shp[q] = jnp.broadcast_to(column, (MEMB, 128))
        mean = jnp.sum(sums, axis=1, keepdims=True) / COUNT
        var = jnp.sum(squares, axis=1, keepdims=True) / COUNT - mean * mean
        scale = jnp.sqrt(var + 1e-05)

        @pl.loop(0, POP // 2)
        def _(t):
            out = pl.ds(pl.multiple_of(t * 48, 48), 48)
            two = (2 * t, 2 * t + 1)
            for h in range(2):
                part = slice(h * MEMB, (h + 1) * MEMB)
                scaled[h, out, :] = jnp.concatenate(
                    [(shp[q][:, 0:1] - mean) / scale * cbuf[q].astype(jnp.float32)[part] / math.sqrt(COUNT) for q in two],
                    axis=0,
                ).astype(jnp.bfloat16)
        left = jnp.transpose(rfull[...]).astype(jnp.bfloat16)
        for h in range(2):
            part = slice(h * HALF, (h + 1) * HALF)
            d = jnp.dot(left, scaled[h], preferred_element_type=jnp.float32)
            neww[:, part] = (wbuf[p, h].astype(jnp.float32) + 0.5 * d).astype(jnp.bfloat16)

    steps = {
        "W": take_w, "C": take_c, "T": take_t, "I": rest_of_own, "Z": start_z, "R": start_r,
        "A": gather_first, "E": gather_near, "K": gather_far, "G": lambda i, j: gather(src[i, j]), "D": delta, "S": take_s,
    }
    for step in ORDER:
        steps[step[0]](*step[1:])
    for s in (1, 0):
        copies["W", 2, 2, s].wait_recv()

        f = src[2, 2]
        h = (acc[s] + jnp.dot(tbuf[f], wbuf[f, s], preferred_element_type=jnp.float32)) / math.sqrt(D)
        keys[:, s * HALF:(s + 1) * HALF] = (jnp.maximum(h, 0.0) ** 2).astype(jnp.bfloat16)

    for copy in copies.values():
        copy.wait_send()

    @pl.when(p == m)
    def _():
        for copy in pieces():
            copy.wait_send()


def local(tokens, weight, fitness, row_factors, col_factors):
    hbm = pl.BlockSpec(memory_space=pl.ANY)
    vmem = pl.BlockSpec(memory_space=pltpu.VMEM)
    bf, f32 = jnp.bfloat16, jnp.float32
    return pl.pallas_call(
        kernel,
        out_shape=(pltpu.VMEM((ROWS, HID), bf), pltpu.VMEM((FEAT, HID), bf)),
        in_specs=[hbm, hbm, pl.BlockSpec(memory_space=pltpu.SMEM), hbm, hbm],
        out_specs=(vmem, vmem),
        scratch_shapes=[
            pltpu.VMEM((MEMB, D), bf),
            pltpu.VMEM((MEMB, HID), bf),
            pltpu.VMEM((POP, 2, FEAT, HALF), bf),
            pltpu.VMEM((2 * NZ, ROWS, FEAT), bf),
            pltpu.VMEM((POP, 2 * MEMB, HALF), bf),
            pltpu.VMEM((POP, 32, FEAT), bf),
            pltpu.VMEM((POP, 32, FEAT), bf),
            pltpu.VMEM((2 * MEMB, HALF), bf),
            pltpu.VMEM((POP, MEMB, FEAT), f32),
            pltpu.VMEM((2, MEMB, HALF), f32),
            pltpu.VMEM((POP, MEMB, 128), f32),
            pltpu.VMEM((2, COUNT, HALF), bf),
            pltpu.VMEM((COUNT, FEAT), f32),
            pltpu.VMEM((2, ROWS, HALF), f32),
            pltpu.VMEM((ROWS, 128), f32),
            pltpu.SemaphoreType.DMA((135,)),
            pltpu.SemaphoreType.DMA((121,)),
            pltpu.SemaphoreType.DMA((5,)),
            pltpu.SemaphoreType.REGULAR((2,)),
        ],
        compiler_params=pltpu.CompilerParams(
            collective_id=0, has_side_effects=True, vmem_limit_bytes=57 << 20
        ),
        cost_estimate=pl.CostEstimate(flops=6_700_000_000, bytes_accessed=4_000_000, transcendentals=0),
    )(tokens, weight, fitness, row_factors, col_factors)


def solution(mesh):
    placed = (P("pop", "mp"), P("pop", "mp"), P("pop"), P("pop", None), P("pop", "mp"))
    return jax.shard_map(
        local,
        mesh=mesh,
        in_specs=placed,
        out_specs=(P("pop", "mp"), P("pop", "mp")),
        check_vma=False,
    )
```

```python
import math

import jax
import jax.numpy as jnp
from jax import lax
from jax.experimental import pallas as pl
from jax.experimental.pallas import tpu as pltpu
from jax.sharding import PartitionSpec as P

D = 4096
N = 4
NZ = 8
POP = N * N
MEMB = 24
TOK = 32
ROWS = MEMB * TOK
FEAT = 256
HID = 1024
HALF = HID // 2
COUNT = POP * MEMB
MESH = pl.DeviceIdType.MESH

ORDER = (
    ("C", 1, 0, 0), ("C", 3, 0, 0), ("C", 0, 1, 0), ("C", 0, 3, 0),
    ("I",), ("Z",), ("R",),
    ("W", 1, 0, 0), ("W", 3, 0, 1), ("W", 0, 1, 0), ("W", 0, 3, 1),
    ("C", 2, 0, 0), ("C", 2, 0, 1), ("C", 1, 1, 0), ("C", 1, 3, 0),
    ("C", 3, 1, 0), ("C", 3, 3, 0), ("C", 0, 2, 0), ("C", 0, 2, 1),
    ("T", 1, 0),
    ("W", 3, 0, 0), ("W", 1, 0, 1), ("W", 0, 1, 1), ("W", 0, 3, 0),
    ("T", 1, 1),
    ("W", 2, 0, 1), ("W", 2, 0, 0),
    ("T", 2, 0), ("S", 1),
    ("W", 1, 1, 0), ("W", 1, 3, 0), ("W", 3, 1, 1), ("W", 3, 3, 1),
    ("T", 2, 1),
    ("W", 0, 2, 0), ("W", 0, 2, 1),
    ("C", 2, 1, 0), ("C", 2, 3, 0), ("C", 1, 2, 1), ("C", 1, 2, 0),
    ("C", 3, 2, 1), ("C", 3, 2, 0),
    ("S", 2), ("A", 0), ("A", 2), ("A", 4),
    ("T", 3, 0),
    ("A", 6), ("A", 8), ("A", 10),
    ("W", 3, 3, 0), ("W", 3, 1, 0), ("A", 12), ("A", 14), ("W", 1, 3, 1), ("W", 1, 1, 1),
    ("T", 3, 1), ("S", 3), ("E", 0),
    ("W", 2, 3, 1), ("W", 2, 1, 1), ("E", 2), ("E", 4),
    ("T", 4, 0), ("E", 6), ("E", 8),
    ("W", 2, 3, 0), ("W", 2, 1, 0), ("E", 10), ("E", 12), ("E", 14), ("S", 4), ("K",),
    ("W", 3, 2, 1), ("W", 1, 2, 0),
    ("G", 2, 1), ("G", 2, 3),
    ("C", 2, 2, 1), ("C", 2, 2, 0),
    ("W", 1, 2, 1), ("W", 3, 2, 0),
    ("D",),
    ("G", 1, 2), ("G", 3, 2),
)


def kernel(tok, w, fit, row_in, col_in, keys, neww,
           row, col, wbuf, tbuf, cbuf, rbuf, rsrc, csrc, rowf, colf, shp, scaled, rfull,
           acc, pacc, ssem, rsem, lsem, ready):
    p, m = lax.axis_index("pop"), lax.axis_index("mp")
    x, y, z, c = lax.rem(p, N), lax.div(p, N), lax.div(m, 2), lax.rem(m, 2)
    a, b = x * (1 - c) + y * c, y * (1 - c) + x * c

    def group(ga, gb):
        ga, gb = lax.rem(ga, N), lax.rem(gb, N)
        return (gb * (1 - c) + ga * c) * N + ga * (1 - c) + gb * c

    def plane(dz, dc=0):
        return lax.rem(z + dz + NZ, NZ) * 2 + lax.rem(c + dc, 2)

    src = {(i, j): group(a + N - i, b + N - j) for i in range(N) for j in range(N)}
    links = {
        "a+": (group(a + 1, b), m), "a-": (group(a + 3, b), m),
        "b+": (group(a, b + 1), m), "b-": (group(a, b + 3), m),
        "z+": (p, plane(1)), "z-": (p, plane(-1)), "s": (p, plane(0, 1)),
    }
    far = [(i, j) for i in range(N) for j in range(N) if (i, j) != (0, 0)]

    def own_w(half):
        return w.at[:, pl.ds(half * HALF, HALF)]

    loads = [
        pltpu.make_async_copy(col_in, col, lsem.at[0]),
        pltpu.make_async_copy(row_in, row, lsem.at[1]),
        pltpu.make_async_copy(own_w(0), wbuf.at[p, 0], lsem.at[2]),
        pltpu.make_async_copy(own_w(1), wbuf.at[p, 1], lsem.at[3]),
        pltpu.make_async_copy(tok, tbuf.at[m], lsem.at[4]),
    ]
    for copy in loads:
        copy.start()

    barrier = pltpu.get_barrier_semaphore()

    def signal(sem, dev):
        pl.semaphore_signal(sem, inc=1, device_id=dev, device_id_type=MESH)

    signal(barrier, links["s"])
    for link in ("a+", "a-", "b+", "b-"):
        signal(barrier, (links[link][0], 2 * z))
    for q in range(2):
        @pl.when(p != 2 * z + q)
        def _(q=q):
            signal(barrier, (2 * z + q, 2 * z))
    for dz in (1, -1):
        signal(barrier, (p, lax.rem(z + dz + NZ, NZ) * 2 + 1))
    source = jnp.where(lax.div(p, 2) == z, 1, 0)

    loads[0].wait()
    colv = col[...].astype(jnp.float32)
    colf[0] = colv[:, :HALF]
    colf[1] = colv[:, HALF:]
    own_col = jnp.concatenate([colv[:, :HALF], colv[:, HALF:]], axis=0).astype(jnp.bfloat16)
    csrc[...] = own_col
    cbuf[p] = own_col

    @pl.when(c == 0)
    def _():
        pl.semaphore_wait(barrier, 9 + 30 * source)
        signal(ready.at[0], links["s"])

    @pl.when(c == 1)
    def _():
        pl.semaphore_wait(ready.at[0], 1)

    copies = {}

    def send(key, source, target, dev):
        n = len(copies)
        copy = pltpu.make_async_remote_copy(
            src_ref=source, dst_ref=target, send_sem=ssem.at[n], recv_sem=rsem.at[n],
            device_id=dev, device_id_type=MESH,
        )
        copy.start()
        copies[key] = copy

    def send_w(link, key, half, source=None):
        slot = src[back(key, link)]
        source = wbuf.at[slot, half] if source is None else source
        send(("W", *key, half), source, wbuf.at[slot, half], links[link])

    def back(key, link):
        i, j = key
        step = {"a+": (1, 0), "a-": (3, 0), "b+": (0, 1), "b-": (0, 3)}[link]
        return ((i - step[0]) % N, (j - step[1]) % N)

    def send_c(link, key, part, lo=0, rows=2 * MEMB):
        slot = src[back(key, link)]
        source = csrc if back(key, link) == (0, 0) else cbuf.at[slot]
        send(("C", *key, part), source.at[pl.ds(lo, rows)], cbuf.at[slot, pl.ds(lo, rows)], links[link])

    send_c("a+", (1, 0), 0)
    send_c("a-", (3, 0), 0)
    send_c("b+", (0, 1), 0)
    send_c("b-", (0, 3), 0)
    send_w("a+", (1, 0), 0, own_w(0))
    send_w("a-", (3, 0), 1, own_w(1))
    send_w("b+", (0, 1), 0, own_w(0))
    send_w("b-", (0, 3), 1, own_w(1))

    send(("S", 0), tok, tbuf.at[m], links["s"])

    loads[1].wait()
    for q in range(POP):
        rowf[q] = row[:, q * FEAT:(q + 1) * FEAT].astype(jnp.float32)

    def pieces(some=far):
        return [
            pltpu.make_async_remote_copy(
                src_ref=rsrc.at[group(a + i, b + j)], dst_ref=rbuf.at[m],
                send_sem=ssem.at[120 + n], recv_sem=rsem.at[120],
                device_id=(group(a + i, b + j), m), device_id_type=MESH,
            )
            for n, (i, j) in enumerate(some)
        ]

    @pl.when(p == m)
    def _():
        lane = lax.broadcasted_iota(jnp.int32, (8, FEAT), 1)
        sub = lax.broadcasted_iota(jnp.int32, (8, FEAT), 0)
        value = jnp.zeros((8, FEAT), jnp.float32)
        for i in range(MEMB):
            value = jnp.where(lane == i, fit[i], value)
        high = value.astype(jnp.bfloat16).astype(jnp.float32)
        middle = (value - high).astype(jnp.bfloat16).astype(jnp.float32)
        low = value - high - middle
        tile = jnp.where(sub == 0, high, jnp.where(sub == 1, middle, jnp.where(sub == 2, low, 0.0)))
        for q in range(POP):
            rsrc[q] = jnp.concatenate([rowf[q], tile], axis=0).astype(jnp.bfloat16)
        for copy in pieces():
            copy.start()
        rbuf[m] = rsrc[p]

    pacc[...] = jnp.zeros_like(pacc)
    acc[...] = jnp.zeros_like(acc)
    for copy in loads[2:]:
        copy.wait()

    def project(blocks):
        @pl.loop(0, MEMB)
        def _(k):
            rows = pl.ds(pl.multiple_of(k * TOK, TOK), TOK)
            total = pacc[rows, :]
            for f in blocks:
                term = tbuf[f, rows, :].astype(jnp.float32) * rowf[f, pl.ds(k, 1), :]
                total = total + (term[:, :128] + term[:, 128:])
            pacc[rows, :] = total

    def half(k):
        return pl.ds(k * (ROWS // 2), ROWS // 2)

    def send_t(dz, k, f=None):
        f = m if f is None else f
        source = tok if abs(dz) == 1 else tbuf.at[f]
        send(("T", dz, k), source.at[half(k)], tbuf.at[f, half(k)], links["z+" if dz > 0 else "z-"])

    def take_t(d, turn):
        for way in (1, -1):
            dz, k = d * way, turn if way > 0 else 1 - turn
            f = plane(-dz)
            copies["T", dz, k].wait_recv()
            if d < 3 or (d == 3 and turn == 0):
                send_t(dz + way, k, f)
            send(("S", dz, k), tbuf.at[f, half(k)], tbuf.at[f, half(k)], links["s"])
            if turn == 1 or (d == 4 and way > 0):
                copies["R", dz].wait_recv()
                if d < 3 or (d == 3 and way > 0):
                    send(("R", dz + way), rbuf.at[f], rbuf.at[f], links["z+" if way > 0 else "z-"])
                send(("Q", dz), rbuf.at[f], rbuf.at[f], links["s"])

    def take_s(d):
        if d == 1:
            copies["S", 0].wait_recv()
            project([m, plane(0, 1)])
        if d < 4:
            for dz in (d, -d):
                for k in range(2):
                    copies["S", dz, k].wait_recv()
            project([plane(-dz, dc) for dz in (d, -d) for dc in (0, 1)])
        else:
            copies["S", 4, 0].wait_recv()
            copies["S", -4, 1].wait_recv()
            project([plane(4), plane(4, 1)])

            @pl.loop(0, MEMB)
            def _(k):
                rows = pl.ds(pl.multiple_of(k * TOK, TOK), TOK)
                proj = 0.3 * jnp.sum(pacc[rows, :], axis=1, keepdims=True)
                for s in range(2):
                    acc[s, rows, :] += proj * colf[s, pl.ds(k, 1), :]

    def take_w(i, j, s):
        copies["W", i, j, s].wait_recv()
        if j == 0:
            if (i, s) == (1, 0):
                send_w("a+", (2, 0), 0)
            if (i, s) == (3, 1):
                send_w("a-", (2, 0), 1)
            send_w("b+", (i, 1), s)
            send_w("b-", (i, 3), s)
        elif (j, s) == (1, 0):
            send_w("b+", (i, 2), 0)
        elif (j, s) == (3, 1):
            send_w("b-", (i, 2), 1)

    def take_c(i, j, part):
        copies["C", i, j, part].wait_recv()
        if j == 0:
            if i == 1:
                send_c("a+", (2, 0), 0, 0, 32)
            if i == 3:
                send_c("a-", (2, 0), 1, 32, 16)
            if i != 2 or part == 1:
                send_c("b+", (i, 1), 0)
                send_c("b-", (i, 3), 0)
        elif j == 1:
            send_c("b+", (i, 2), 0, 0, 16 if i in (0, 2) else 32)
        elif j == 3:
            lo = 16 if i in (0, 2) else 32
            send_c("b-", (i, 2), 1, lo, 48 - lo)

    def gather(f):
        for s in range(2):
            acc[s] += jnp.dot(tbuf[f], wbuf[f, s], preferred_element_type=jnp.float32)

    def place(f):
        fx, fy = lax.rem(f, N), lax.div(f, N)
        i = lax.rem(a + N - (fx * (1 - c) + fy * c), N)
        j = lax.rem(b + N - (fy * (1 - c) + fx * c), N)
        dz = lax.rem(lax.div(f, 2) + NZ - z, NZ)
        return i, j, jnp.minimum(dz, NZ - dz)

    def early(f):
        i, j, _ = place(f)
        return (i == 0) | (j == 0) | ((i != 2) & (j != 2))

    def first(f):
        i, j, d = place(f)
        return (((i == 0) & (j != 2)) | (j == 0)) & (d <= 2)

    def gather_first(start):
        @pl.loop(start, start + 2)
        def _(f):
            @pl.when(first(f))
            def _():
                gather(f)

    def gather_near(start):
        @pl.loop(start, start + 2)
        def _(f):
            @pl.when(early(f) & jnp.logical_not(first(f)) & (place(f)[2] <= 3))
            def _():
                gather(f)

    def gather_far():
        for dc in range(2):
            f = plane(4, dc)

            @pl.when(early(f))
            def _(f=f):
                gather(f)

    def start_z():
        @pl.when(c == 1)
        def _():
            pl.semaphore_wait(barrier, 5)
            signal(ready.at[1], links["s"])

        @pl.when(c == 0)
        def _():
            pl.semaphore_wait(ready.at[1], 1)

        for turn in range(2):
            send_t(1, turn)
            send_t(-1, 1 - turn)

    def start_r():
        @pl.when(p != m)
        def _():
            pieces(far[:1])[0].wait_recv()

        for dz, link in ((1, "z+"), (-1, "z-")):
            send(("R", dz), rbuf.at[m], rbuf.at[m], links[link])
        send(("Q", 0), rbuf.at[m], rbuf.at[m], links["s"])

    def rest_of_own():
        send_w("a+", (1, 0), 1, own_w(1))
        send_w("a-", (3, 0), 0, own_w(0))
        send_w("b+", (0, 1), 1, own_w(1))
        send_w("b-", (0, 3), 0, own_w(0))

    def delta():
        for dz in (0, 1, -1, 2, -2, 3, -3, 4):
            copies["Q", dz].wait_recv()
        diagonal = lax.broadcasted_iota(jnp.int32, (MEMB, 128), 0) == lax.broadcasted_iota(jnp.int32, (MEMB, 128), 1)
        sums = jnp.zeros((1, 128), jnp.float32)
        squares = jnp.zeros((1, 128), jnp.float32)
        for q in range(POP):
            piece = rbuf[q].astype(jnp.float32)
            rfull[q * MEMB:(q + 1) * MEMB, :] = piece[:MEMB]
            tail = piece[MEMB:, :128]
            value = (tail[0:1] + tail[1:2]) + tail[2:3]
            sums += value
            squares += value * value
            column = jnp.sum(jnp.where(diagonal, value, 0.0), axis=1, keepdims=True)
            shp[q] = jnp.broadcast_to(column, (MEMB, 128))
        mean = jnp.sum(sums, axis=1, keepdims=True) / COUNT
        var = jnp.sum(squares, axis=1, keepdims=True) / COUNT - mean * mean
        scale = jnp.sqrt(var + 1e-05)

        @pl.loop(0, POP // 2)
        def _(t):
            out = pl.ds(pl.multiple_of(t * 48, 48), 48)
            two = (2 * t, 2 * t + 1)
            for h in range(2):
                part = slice(h * MEMB, (h + 1) * MEMB)
                scaled[h, out, :] = jnp.concatenate(
                    [(shp[q][:, 0:1] - mean) / scale * cbuf[q].astype(jnp.float32)[part] / math.sqrt(COUNT) for q in two],
                    axis=0,
                ).astype(jnp.bfloat16)
        left = jnp.transpose(rfull[...]).astype(jnp.bfloat16)
        for h in range(2):
            part = slice(h * HALF, (h + 1) * HALF)
            d = jnp.dot(left, scaled[h], preferred_element_type=jnp.float32)
            neww[:, part] = (wbuf[p, h].astype(jnp.float32) + 0.5 * d).astype(jnp.bfloat16)

    steps = {
        "W": take_w, "C": take_c, "T": take_t, "I": rest_of_own, "Z": start_z, "R": start_r,
        "A": gather_first, "E": gather_near, "K": gather_far, "G": lambda i, j: gather(src[i, j]), "D": delta, "S": take_s,
    }
    for step in ORDER:
        steps[step[0]](*step[1:])
    for s in (1, 0):
        copies["W", 2, 2, s].wait_recv()

        f = src[2, 2]
        h = (acc[s] + jnp.dot(tbuf[f], wbuf[f, s], preferred_element_type=jnp.float32)) / math.sqrt(D)
        keys[:, s * HALF:(s + 1) * HALF] = (jnp.maximum(h, 0.0) ** 2).astype(jnp.bfloat16)

    for copy in copies.values():
        copy.wait_send()

    @pl.when(p == m)
    def _():
        for copy in pieces():
            copy.wait_send()


def local(tokens, weight, fitness, row_factors, col_factors):
    hbm = pl.BlockSpec(memory_space=pl.ANY)
    vmem = pl.BlockSpec(memory_space=pltpu.VMEM)
    bf, f32 = jnp.bfloat16, jnp.float32
    return pl.pallas_call(
        kernel,
        out_shape=(pltpu.VMEM((ROWS, HID), bf), pltpu.VMEM((FEAT, HID), bf)),
        in_specs=[hbm, hbm, pl.BlockSpec(memory_space=pltpu.SMEM), hbm, hbm],
        out_specs=(vmem, vmem),
        scratch_shapes=[
            pltpu.VMEM((MEMB, D), bf),
            pltpu.VMEM((MEMB, HID), bf),
            pltpu.VMEM((POP, 2, FEAT, HALF), bf),
            pltpu.VMEM((2 * NZ, ROWS, FEAT), bf),
            pltpu.VMEM((POP, 2 * MEMB, HALF), bf),
            pltpu.VMEM((POP, 32, FEAT), bf),
            pltpu.VMEM((POP, 32, FEAT), bf),
            pltpu.VMEM((2 * MEMB, HALF), bf),
            pltpu.VMEM((POP, MEMB, FEAT), f32),
            pltpu.VMEM((2, MEMB, HALF), f32),
            pltpu.VMEM((POP, MEMB, 128), f32),
            pltpu.VMEM((2, COUNT, HALF), bf),
            pltpu.VMEM((COUNT, FEAT), f32),
            pltpu.VMEM((2, ROWS, HALF), f32),
            pltpu.VMEM((ROWS, 128), f32),
            pltpu.SemaphoreType.DMA((135,)),
            pltpu.SemaphoreType.DMA((121,)),
            pltpu.SemaphoreType.DMA((5,)),
            pltpu.SemaphoreType.REGULAR((2,)),
        ],
        compiler_params=pltpu.CompilerParams(
            collective_id=0, has_side_effects=True, vmem_limit_bytes=57 << 20
        ),
        cost_estimate=pl.CostEstimate(flops=6_700_000_000, bytes_accessed=4_000_000, transcendentals=0),
    )(tokens, weight, fitness, row_factors, col_factors)


def solution(mesh):
    placed = (P("pop", "mp"), P("pop", "mp"), P("pop"), P("pop", None), P("pop", "mp"))
    return jax.shard_map(
        local,
        mesh=mesh,
        in_specs=placed,
        out_specs=(P("pop", "mp"), P("pop", "mp")),
        check_vma=False,
    )
```

```python
import math

import jax
import jax.numpy as jnp
from jax import lax
from jax.experimental import pallas as pl
from jax.experimental.pallas import tpu as pltpu
from jax.sharding import PartitionSpec as P

D = 4096
N = 4
NZ = 8
POP = N * N
MEMB = 24
TOK = 32
ROWS = MEMB * TOK
FEAT = 256
HID = 1024
HALF = HID // 2
COUNT = POP * MEMB
MESH = pl.DeviceIdType.MESH

ORDER = (
    ("C", 1, 0, 0), ("C", 3, 0, 0), ("C", 0, 1, 0), ("C", 0, 3, 0), ("I",), ("Z",), ("R",), ("W", 1, 0, 0),
    ("W", 3, 0, 1), ("W", 0, 1, 0), ("W", 0, 3, 1), ("C", 2, 0, 0), ("C", 2, 0, 1), ("C", 1, 1, 0),
    ("C", 1, 3, 0), ("C", 3, 1, 0), ("C", 3, 3, 0), ("C", 0, 2, 0), ("C", 0, 2, 1), ("T", 1, 0),
    ("W", 3, 0, 0), ("W", 1, 0, 1), ("W", 0, 1, 1), ("T", 1, 1), ("W", 0, 3, 0), ("S", 1), ("W", 2, 0, 1),
    ("W", 2, 0, 0), ("T", 2, 0), ("W", 1, 1, 0), ("W", 1, 3, 0), ("W", 3, 1, 1), ("W", 3, 3, 1), ("T", 2, 1),
    ("W", 0, 2, 0), ("W", 0, 2, 1), ("S", 2), ("A", 0), ("C", 2, 1, 0), ("C", 2, 3, 0), ("C", 1, 2, 1),
    ("C", 1, 2, 0), ("C", 3, 2, 1), ("A", 2), ("C", 3, 2, 0), ("A", 4), ("T", 3, 0), ("A", 6), ("W", 3, 3, 0),
    ("A", 8), ("W", 3, 1, 0), ("A", 10), ("A", 12), ("W", 1, 3, 1), ("A", 14), ("T", 3, 1), ("W", 1, 1, 1),
    ("B", 0), ("B", 2), ("B", 4), ("S", 3), ("B", 6), ("W", 2, 3, 1), ("B", 8), ("W", 2, 1, 1), ("B", 10),
    ("B", 12), ("T", 4, 0), ("B", 14), ("K", 3), ("W", 2, 3, 0), ("W", 2, 1, 0), ("K", -3), ("S", 4),
    ("K", 4), ("G", 2, 1), ("W", 3, 2, 1), ("W", 1, 2, 0), ("C", 2, 2, 1), ("G", 2, 3), ("C", 2, 2, 0),
    ("D",), ("W", 1, 2, 1), ("W", 3, 2, 0), ("G", 1, 2), ("G", 3, 2),
)


def kernel(tok, w, fit, row_in, col_in, keys, neww,
           row, col, wbuf, tbuf, cbuf, rbuf, rsrc, csrc, rowf, colf, shp, scaled, rfull,
           acc, pacc, ssem, rsem, lsem, ready):
    p, m = lax.axis_index("pop"), lax.axis_index("mp")
    x, y, z, c = lax.rem(p, N), lax.div(p, N), lax.div(m, 2), lax.rem(m, 2)
    a, b = x * (1 - c) + y * c, y * (1 - c) + x * c

    def group(ga, gb):
        ga, gb = lax.rem(ga, N), lax.rem(gb, N)
        return (gb * (1 - c) + ga * c) * N + ga * (1 - c) + gb * c

    def plane(dz, dc=0):
        return lax.rem(z + dz + NZ, NZ) * 2 + lax.rem(c + dc, 2)

    src = {(i, j): group(a + N - i, b + N - j) for i in range(N) for j in range(N)}
    links = {
        "a+": (group(a + 1, b), m), "a-": (group(a + 3, b), m),
        "b+": (group(a, b + 1), m), "b-": (group(a, b + 3), m),
        "z+": (p, plane(1)), "z-": (p, plane(-1)), "s": (p, plane(0, 1)),
    }
    far = [(i, j) for i in range(N) for j in range(N) if (i, j) != (0, 0)]

    def own_w(half):
        return w.at[:, pl.ds(half * HALF, HALF)]

    loads = [
        pltpu.make_async_copy(col_in, col, lsem.at[0]),
        pltpu.make_async_copy(row_in, row, lsem.at[1]),
        pltpu.make_async_copy(own_w(0), wbuf.at[p, 0], lsem.at[2]),
        pltpu.make_async_copy(own_w(1), wbuf.at[p, 1], lsem.at[3]),
        pltpu.make_async_copy(tok, tbuf.at[m], lsem.at[4]),
    ]
    for copy in loads:
        copy.start()

    barrier = pltpu.get_barrier_semaphore()

    def signal(sem, dev):
        pl.semaphore_signal(sem, inc=1, device_id=dev, device_id_type=MESH)

    signal(barrier, links["s"])
    for link in ("a+", "a-", "b+", "b-"):
        signal(barrier, (links[link][0], 2 * z))
    for q in range(2):
        @pl.when(p != 2 * z + q)
        def _(q=q):
            signal(barrier, (2 * z + q, 2 * z))
    for dz in (1, -1):
        signal(barrier, (p, lax.rem(z + dz + NZ, NZ) * 2 + 1))
    source = jnp.where(lax.div(p, 2) == z, 1, 0)

    loads[0].wait()
    colv = col[...].astype(jnp.float32)
    colf[0] = colv[:, :HALF]
    colf[1] = colv[:, HALF:]
    own_col = jnp.concatenate([colv[:, :HALF], colv[:, HALF:]], axis=0).astype(jnp.bfloat16)
    csrc[...] = own_col
    cbuf[p] = own_col

    for copy in loads[2:]:
        copy.wait()

    @pl.when(c == 0)
    def _():
        pl.semaphore_wait(barrier, 9 + 30 * source)
        signal(ready.at[0], links["s"])

    @pl.when(c == 1)
    def _():
        pl.semaphore_wait(ready.at[0], 1)

    copies = {}

    def send(key, source, target, dev):
        n = len(copies)
        copy = pltpu.make_async_remote_copy(
            src_ref=source, dst_ref=target, send_sem=ssem.at[n], recv_sem=rsem.at[n],
            device_id=dev, device_id_type=MESH,
        )
        copy.start()
        copies[key] = copy

    def send_w(link, key, half, source=None):
        slot = src[back(key, link)]
        source = wbuf.at[slot, half]
        send(("W", *key, half), source, wbuf.at[slot, half], links[link])

    def back(key, link):
        i, j = key
        step = {"a+": (1, 0), "a-": (3, 0), "b+": (0, 1), "b-": (0, 3)}[link]
        return ((i - step[0]) % N, (j - step[1]) % N)

    def send_c(link, key, part, lo=0, rows=2 * MEMB):
        slot = src[back(key, link)]
        source = csrc if back(key, link) == (0, 0) else cbuf.at[slot]
        send(("C", *key, part), source.at[pl.ds(lo, rows)], cbuf.at[slot, pl.ds(lo, rows)], links[link])

    send_c("a+", (1, 0), 0)
    send_c("a-", (3, 0), 0)
    send_c("b+", (0, 1), 0)
    send_c("b-", (0, 3), 0)
    send_w("a+", (1, 0), 0, own_w(0))
    send_w("a-", (3, 0), 1, own_w(1))
    send_w("b+", (0, 1), 0, own_w(0))
    send_w("b-", (0, 3), 1, own_w(1))

    send(("S", 0), tbuf.at[m], tbuf.at[m], links["s"])

    loads[1].wait()
    for q in range(POP):
        rowf[q] = row[:, q * FEAT:(q + 1) * FEAT].astype(jnp.float32)

    def pieces(some=far):
        return [
            pltpu.make_async_remote_copy(
                src_ref=rsrc.at[group(a + i, b + j)], dst_ref=rbuf.at[m],
                send_sem=ssem.at[120 + n], recv_sem=rsem.at[120],
                device_id=(group(a + i, b + j), m), device_id_type=MESH,
            )
            for n, (i, j) in enumerate(some)
        ]

    @pl.when(p == m)
    def _():
        lane = lax.broadcasted_iota(jnp.int32, (8, FEAT), 1)
        sub = lax.broadcasted_iota(jnp.int32, (8, FEAT), 0)
        value = jnp.zeros((8, FEAT), jnp.float32)
        for i in range(MEMB):
            value = jnp.where(lane == i, fit[i], value)
        high = value.astype(jnp.bfloat16).astype(jnp.float32)
        middle = (value - high).astype(jnp.bfloat16).astype(jnp.float32)
        low = value - high - middle
        tile = jnp.where(sub == 0, high, jnp.where(sub == 1, middle, jnp.where(sub == 2, low, 0.0)))
        for q in range(POP):
            rsrc[q] = jnp.concatenate([rowf[q], tile], axis=0).astype(jnp.bfloat16)
        for copy in pieces():
            copy.start()
        rbuf[m] = rsrc[p]

    pacc[...] = jnp.zeros_like(pacc)
    acc[...] = jnp.zeros_like(acc)

    def project(blocks):
        @pl.loop(0, MEMB)
        def _(k):
            rows = pl.ds(pl.multiple_of(k * TOK, TOK), TOK)
            total = pacc[rows, :]
            for f in blocks:
                term = tbuf[f, rows, :].astype(jnp.float32) * rowf[f, pl.ds(k, 1), :]
                total = total + (term[:, :128] + term[:, 128:])
            pacc[rows, :] = total

    def half(k):
        return pl.ds(k * (ROWS // 2), ROWS // 2)

    def send_t(dz, k, f=None):
        f = m if f is None else f
        source = tbuf.at[f]
        send(("T", dz, k), source.at[half(k)], tbuf.at[f, half(k)], links["z+" if dz > 0 else "z-"])

    def take_t(d, turn):
        for way in (1, -1):
            dz, k = d * way, turn if way > 0 else 1 - turn
            f = plane(-dz)
            copies["T", dz, k].wait_recv()
            if d < 3 or (d == 3 and turn == 0):
                send_t(dz + way, k, f)
            send(("S", dz, k), tbuf.at[f, half(k)], tbuf.at[f, half(k)], links["s"])
            if turn == 1 or (d == 4 and way > 0):
                copies["R", dz].wait_recv()
                if d < 3 or (d == 3 and way > 0):
                    send(("R", dz + way), rbuf.at[f], rbuf.at[f], links["z+" if way > 0 else "z-"])
                send(("Q", dz), rbuf.at[f], rbuf.at[f], links["s"])

    def take_s(d):
        if d == 1:
            copies["S", 0].wait_recv()
            project([m, plane(0, 1)])
        if d < 4:
            for dz in (d, -d):
                for k in range(2):
                    copies["S", dz, k].wait_recv()
            project([plane(-dz, dc) for dz in (d, -d) for dc in (0, 1)])
        else:
            copies["S", 4, 0].wait_recv()
            copies["S", -4, 1].wait_recv()
            project([plane(4), plane(4, 1)])

            @pl.loop(0, MEMB)
            def _(k):
                rows = pl.ds(pl.multiple_of(k * TOK, TOK), TOK)
                proj = 0.3 * jnp.sum(pacc[rows, :], axis=1, keepdims=True)
                for s in range(2):
                    acc[s, rows, :] += proj * colf[s, pl.ds(k, 1), :]

    def take_w(i, j, s):
        copies["W", i, j, s].wait_recv()
        if j == 0:
            if (i, s) == (1, 0):
                send_w("a+", (2, 0), 0)
            if (i, s) == (3, 1):
                send_w("a-", (2, 0), 1)
            send_w("b+", (i, 1), s)
            send_w("b-", (i, 3), s)
        elif (j, s) == (1, 0):
            send_w("b+", (i, 2), 0)
        elif (j, s) == (3, 1):
            send_w("b-", (i, 2), 1)

    def take_c(i, j, part):
        copies["C", i, j, part].wait_recv()
        if j == 0:
            if i == 1:
                send_c("a+", (2, 0), 0, 0, 32)
            if i == 3:
                send_c("a-", (2, 0), 1, 32, 16)
            if i != 2 or part == 1:
                send_c("b+", (i, 1), 0)
                send_c("b-", (i, 3), 0)
        elif j == 1:
            send_c("b+", (i, 2), 0, 0, 16 if i in (0, 2) else 32)
        elif j == 3:
            lo = 16 if i in (0, 2) else 32
            send_c("b-", (i, 2), 1, lo, 48 - lo)

    def gather(f):
        for s in range(2):
            acc[s] += jnp.dot(tbuf[f], wbuf[f, s], preferred_element_type=jnp.float32)

    def place(f):
        fx, fy = lax.rem(f, N), lax.div(f, N)
        i = lax.rem(a + N - (fx * (1 - c) + fy * c), N)
        j = lax.rem(b + N - (fy * (1 - c) + fx * c), N)
        dz = lax.rem(lax.div(f, 2) + NZ - z, NZ)
        return i, j, jnp.minimum(dz, NZ - dz)

    def early(f):
        i, j, _ = place(f)
        return (i == 0) | (j == 0) | ((i != 2) & (j != 2))

    def first(f):
        i, j, _ = place(f)
        return ((i == 0) & (j != 2)) | (j == 0)

    def gather_first(start):
        @pl.loop(start, start + 2)
        def _(f):
            @pl.when(first(f) & (place(f)[2] <= 2))
            def _():
                gather(f)

    def gather_next(start):
        @pl.loop(start, start + 2)
        def _(f):
            @pl.when(early(f) & jnp.logical_not(first(f)) & (place(f)[2] <= 2))
            def _():
                gather(f)

    def gather_far(dz):
        @pl.loop(0, 2)
        def _(dc):
            f = plane(dz, dc)

            @pl.when(early(f))
            def _():
                gather(f)

    def start_z():
        @pl.when(c == 1)
        def _():
            pl.semaphore_wait(barrier, 5)
            signal(ready.at[1], links["s"])

        @pl.when(c == 0)
        def _():
            pl.semaphore_wait(ready.at[1], 1)

        for turn in range(2):
            send_t(1, turn)
            send_t(-1, 1 - turn)

    def start_r():
        @pl.when(p != m)
        def _():
            pieces(far[:1])[0].wait_recv()

        for dz, link in ((1, "z+"), (-1, "z-")):
            send(("R", dz), rbuf.at[m], rbuf.at[m], links[link])
        send(("Q", 0), rbuf.at[m], rbuf.at[m], links["s"])

    def rest_of_own():
        send_w("a+", (1, 0), 1, own_w(1))
        send_w("a-", (3, 0), 0, own_w(0))
        send_w("b+", (0, 1), 1, own_w(1))
        send_w("b-", (0, 3), 0, own_w(0))

    def delta():
        for dz in (0, 1, -1, 2, -2, 3, -3, 4):
            copies["Q", dz].wait_recv()
        diagonal = lax.broadcasted_iota(jnp.int32, (MEMB, 128), 0) == lax.broadcasted_iota(jnp.int32, (MEMB, 128), 1)
        sums = jnp.zeros((1, 128), jnp.float32)
        squares = jnp.zeros((1, 128), jnp.float32)
        for q in range(POP):
            piece = rbuf[q].astype(jnp.float32)
            rfull[q * MEMB:(q + 1) * MEMB, :] = piece[:MEMB]
            tail = piece[MEMB:, :128]
            value = (tail[0:1] + tail[1:2]) + tail[2:3]
            sums += value
            squares += value * value
            column = jnp.sum(jnp.where(diagonal, value, 0.0), axis=1, keepdims=True)
            shp[q] = jnp.broadcast_to(column, (MEMB, 128))
        mean = jnp.sum(sums, axis=1, keepdims=True) / COUNT
        var = jnp.sum(squares, axis=1, keepdims=True) / COUNT - mean * mean
        scale = jnp.sqrt(var + 1e-05)

        @pl.loop(0, POP // 2)
        def _(t):
            out = pl.ds(pl.multiple_of(t * 48, 48), 48)
            two = (2 * t, 2 * t + 1)
            for h in range(2):
                part = slice(h * MEMB, (h + 1) * MEMB)
                scaled[h, out, :] = jnp.concatenate(
                    [(shp[q][:, 0:1] - mean) / scale * cbuf[q].astype(jnp.float32)[part] / math.sqrt(COUNT) for q in two],
                    axis=0,
                ).astype(jnp.bfloat16)
        left = jnp.transpose(rfull[...]).astype(jnp.bfloat16)
        for h in range(2):
            part = slice(h * HALF, (h + 1) * HALF)
            d = jnp.dot(left, scaled[h], preferred_element_type=jnp.float32)
            neww[:, part] = (wbuf[p, h].astype(jnp.float32) + 0.5 * d).astype(jnp.bfloat16)

    steps = {
        "W": take_w, "C": take_c, "T": take_t, "I": rest_of_own, "Z": start_z, "R": start_r,
        "A": gather_first, "B": gather_next, "K": gather_far, "G": lambda i, j: gather(src[i, j]), "D": delta, "S": take_s,
    }
    for step in ORDER:
        steps[step[0]](*step[1:])
    for s in (1, 0):
        copies["W", 2, 2, s].wait_recv()

        f = src[2, 2]
        h = (acc[s] + jnp.dot(tbuf[f], wbuf[f, s], preferred_element_type=jnp.float32)) / math.sqrt(D)
        keys[:, s * HALF:(s + 1) * HALF] = (jnp.maximum(h, 0.0) ** 2).astype(jnp.bfloat16)

    for copy in copies.values():
        copy.wait_send()

    @pl.when(p == m)
    def _():
        for copy in pieces():
            copy.wait_send()


def local(tokens, weight, fitness, row_factors, col_factors):
    hbm = pl.BlockSpec(memory_space=pl.ANY)
    vmem = pl.BlockSpec(memory_space=pltpu.VMEM)
    bf, f32 = jnp.bfloat16, jnp.float32
    return pl.pallas_call(
        kernel,
        out_shape=(pltpu.VMEM((ROWS, HID), bf), pltpu.VMEM((FEAT, HID), bf)),
        in_specs=[hbm, hbm, pl.BlockSpec(memory_space=pltpu.SMEM), hbm, hbm],
        out_specs=(vmem, vmem),
        scratch_shapes=[
            pltpu.VMEM((MEMB, D), bf),
            pltpu.VMEM((MEMB, HID), bf),
            pltpu.VMEM((POP, 2, FEAT, HALF), bf),
            pltpu.VMEM((2 * NZ, ROWS, FEAT), bf),
            pltpu.VMEM((POP, 2 * MEMB, HALF), bf),
            pltpu.VMEM((POP, 32, FEAT), bf),
            pltpu.VMEM((POP, 32, FEAT), bf),
            pltpu.VMEM((2 * MEMB, HALF), bf),
            pltpu.VMEM((POP, MEMB, FEAT), f32),
            pltpu.VMEM((2, MEMB, HALF), f32),
            pltpu.VMEM((POP, MEMB, 128), f32),
            pltpu.VMEM((2, COUNT, HALF), bf),
            pltpu.VMEM((COUNT, FEAT), f32),
            pltpu.VMEM((2, ROWS, HALF), f32),
            pltpu.VMEM((ROWS, 128), f32),
            pltpu.SemaphoreType.DMA((135,)),
            pltpu.SemaphoreType.DMA((121,)),
            pltpu.SemaphoreType.DMA((5,)),
            pltpu.SemaphoreType.REGULAR((2,)),
        ],
        compiler_params=pltpu.CompilerParams(
            collective_id=0, has_side_effects=True, vmem_limit_bytes=57 << 20
        ),
        cost_estimate=pl.CostEstimate(flops=6_700_000_000, bytes_accessed=4_000_000, transcendentals=0),
    )(tokens, weight, fitness, row_factors, col_factors)


def solution(mesh):
    placed = (P("pop", "mp"), P("pop", "mp"), P("pop"), P("pop", None), P("pop", "mp"))
    return jax.shard_map(
        local,
        mesh=mesh,
        in_specs=placed,
        out_specs=(P("pop", "mp"), P("pop", "mp")),
        check_vma=False,
    )
```

```python
import math

import jax
import jax.numpy as jnp
from jax import lax
from jax.experimental import pallas as pl
from jax.experimental.pallas import tpu as pltpu
from jax.sharding import PartitionSpec as P

D = 4096
N = 4
NZ = 8
POP = N * N
MEMB = 24
TOK = 32
ROWS = MEMB * TOK
FEAT = 256
HID = 1024
HALF = HID // 2
COUNT = POP * MEMB
MESH = pl.DeviceIdType.MESH

ORDER = (
    ("C", 1, 0, 0), ("C", 3, 0, 0), ("C", 0, 1, 0), ("C", 0, 3, 0), ("I",), ("Z",), ("W", 1, 0, 0),
    ("W", 3, 0, 1), ("W", 0, 1, 0), ("W", 0, 3, 1), ("C", 2, 0, 0), ("C", 2, 0, 1), ("C", 1, 1, 0),
    ("C", 1, 3, 0), ("C", 3, 1, 0), ("C", 3, 3, 0), ("C", 0, 2, 0), ("C", 0, 2, 1), ("R",), ("T", 1, 0),
    ("W", 3, 0, 0), ("W", 1, 0, 1), ("W", 0, 1, 1), ("T", 1, 1), ("W", 0, 3, 0), ("S", 1), ("W", 2, 0, 1),
    ("W", 2, 0, 0), ("T", 2, 0), ("W", 1, 1, 0), ("W", 1, 3, 0), ("W", 3, 1, 1), ("W", 3, 3, 1), ("T", 2, 1),
    ("W", 0, 2, 0), ("W", 0, 2, 1), ("S", 2), ("A", 0), ("C", 2, 1, 0), ("C", 2, 3, 0), ("C", 1, 2, 1),
    ("C", 1, 2, 0), ("C", 3, 2, 1), ("A", 2), ("C", 3, 2, 0), ("A", 4), ("T", 3, 0), ("A", 6), ("W", 3, 3, 0),
    ("A", 8), ("W", 3, 1, 0), ("A", 10), ("A", 12), ("W", 1, 3, 1), ("A", 14), ("T", 3, 1), ("W", 1, 1, 1),
    ("B", 0), ("B", 2), ("B", 4), ("S", 3), ("B", 6), ("W", 2, 3, 1), ("B", 8), ("W", 2, 1, 1), ("B", 10),
    ("B", 12), ("F", 30), ("T", 4, 0), ("B", 14), ("K", 3), ("W", 2, 3, 0), ("W", 2, 1, 0), ("K", -3), ("S", 4),
    ("K", 4), ("G", 2, 1), ("W", 3, 2, 1), ("W", 1, 2, 0), ("C", 2, 2, 1), ("G", 2, 3), ("C", 2, 2, 0),
    ("F", 20), ("D",), ("W", 1, 2, 1), ("W", 3, 2, 0), ("G", 1, 2), ("G", 3, 2),
)


def kernel(tok, w, fit, row_in, col_in, keys, neww,
           row, col, wbuf, tbuf, cbuf, rbuf, rsrc, csrc, rowf, colf, shp, scaled, rfull,
           acc, pacc, ssem, rsem, lsem, ready):
    p, m = lax.axis_index("pop"), lax.axis_index("mp")
    x, y, z, c = lax.rem(p, N), lax.div(p, N), lax.div(m, 2), lax.rem(m, 2)
    a, b = x * (1 - c) + y * c, y * (1 - c) + x * c

    def group(ga, gb):
        ga, gb = lax.rem(ga, N), lax.rem(gb, N)
        return (gb * (1 - c) + ga * c) * N + ga * (1 - c) + gb * c

    def plane(dz, dc=0):
        return lax.rem(z + dz + NZ, NZ) * 2 + lax.rem(c + dc, 2)

    src = {(i, j): group(a + N - i, b + N - j) for i in range(N) for j in range(N)}
    links = {
        "a+": (group(a + 1, b), m), "a-": (group(a + 3, b), m),
        "b+": (group(a, b + 1), m), "b-": (group(a, b + 3), m),
        "z+": (p, plane(1)), "z-": (p, plane(-1)), "s": (p, plane(0, 1)),
    }
    far = [(i, j) for i in range(N) for j in range(N) if (i, j) != (0, 0)]

    def own_w(half):
        return w.at[:, pl.ds(half * HALF, HALF)]

    loads = [
        pltpu.make_async_copy(col_in, col, lsem.at[0]),
        pltpu.make_async_copy(row_in, row, lsem.at[1]),
        pltpu.make_async_copy(own_w(0), wbuf.at[p, 0], lsem.at[2]),
        pltpu.make_async_copy(own_w(1), wbuf.at[p, 1], lsem.at[3]),
        pltpu.make_async_copy(tok, tbuf.at[m], lsem.at[4]),
    ]
    for copy in loads:
        copy.start()

    barrier = pltpu.get_barrier_semaphore()

    def signal(sem, dev):
        pl.semaphore_signal(sem, inc=1, device_id=dev, device_id_type=MESH)

    signal(barrier, links["s"])
    for link in ("a+", "a-", "b+", "b-"):
        signal(barrier, (links[link][0], 2 * z))
    for q in range(2):
        @pl.when(p != 2 * z + q)
        def _(q=q):
            signal(barrier, (2 * z + q, 2 * z))
    for dz in (1, -1):
        signal(barrier, (p, lax.rem(z + dz + NZ, NZ) * 2 + 1))
    source = jnp.where(lax.div(p, 2) == z, 1, 0)

    loads[0].wait()
    colv = col[...].astype(jnp.float32)
    colf[0] = colv[:, :HALF]
    colf[1] = colv[:, HALF:]
    own_col = jnp.concatenate([colv[:, :HALF], colv[:, HALF:]], axis=0).astype(jnp.bfloat16)
    csrc[...] = own_col
    cbuf[p] = own_col

    for copy in loads[2:]:
        copy.wait()

    @pl.when(c == 0)
    def _():
        pl.semaphore_wait(barrier, 9 + 30 * source)
        signal(ready.at[0], links["s"])

    @pl.when(c == 1)
    def _():
        pl.semaphore_wait(ready.at[0], 1)

    copies = {}

    def send(key, source, target, dev):
        n = len(copies)
        copy = pltpu.make_async_remote_copy(
            src_ref=source, dst_ref=target, send_sem=ssem.at[n], recv_sem=rsem.at[n],
            device_id=dev, device_id_type=MESH,
        )
        copy.start()
        copies[key] = copy

    def send_w(link, key, half, source=None):
        slot = src[back(key, link)]
        source = wbuf.at[slot, half]
        send(("W", *key, half), source, wbuf.at[slot, half], links[link])

    def back(key, link):
        i, j = key
        step = {"a+": (1, 0), "a-": (3, 0), "b+": (0, 1), "b-": (0, 3)}[link]
        return ((i - step[0]) % N, (j - step[1]) % N)

    def send_c(link, key, part, lo=0, rows=2 * MEMB):
        slot = src[back(key, link)]
        source = csrc if back(key, link) == (0, 0) else cbuf.at[slot]
        send(("C", *key, part), source.at[pl.ds(lo, rows)], cbuf.at[slot, pl.ds(lo, rows)], links[link])

    send_c("a+", (1, 0), 0)
    send_c("a-", (3, 0), 0)
    send_c("b+", (0, 1), 0)
    send_c("b-", (0, 3), 0)
    send_w("a+", (1, 0), 0, own_w(0))
    send_w("a-", (3, 0), 1, own_w(1))
    send_w("b+", (0, 1), 0, own_w(0))
    send_w("b-", (0, 3), 1, own_w(1))

    send(("S", 0), tbuf.at[m], tbuf.at[m], links["s"])

    loads[1].wait()
    for q in range(POP):
        rowf[q] = row[:, q * FEAT:(q + 1) * FEAT].astype(jnp.float32)

    def pieces(some=far):
        return [
            pltpu.make_async_remote_copy(
                src_ref=rsrc.at[group(a + i, b + j)], dst_ref=rbuf.at[m],
                send_sem=ssem.at[120 + n], recv_sem=rsem.at[120],
                device_id=(group(a + i, b + j), m), device_id_type=MESH,
            )
            for n, (i, j) in enumerate(some)
        ]

    @pl.when(p == m)
    def _():
        lane = lax.broadcasted_iota(jnp.int32, (8, FEAT), 1)
        sub = lax.broadcasted_iota(jnp.int32, (8, FEAT), 0)
        value = jnp.zeros((8, FEAT), jnp.float32)
        for i in range(MEMB):
            value = jnp.where(lane == i, fit[i], value)
        high = value.astype(jnp.bfloat16).astype(jnp.float32)
        middle = (value - high).astype(jnp.bfloat16).astype(jnp.float32)
        low = value - high - middle
        tile = jnp.where(sub == 0, high, jnp.where(sub == 1, middle, jnp.where(sub == 2, low, 0.0)))
        for q in range(POP):
            rsrc[q] = jnp.concatenate([rowf[q], tile], axis=0).astype(jnp.bfloat16)
        for copy in pieces():
            copy.start()
        rbuf[m] = rsrc[p]

    pacc[...] = jnp.zeros_like(pacc)
    acc[...] = jnp.zeros_like(acc)

    def project(blocks):
        @pl.loop(0, MEMB)
        def _(k):
            rows = pl.ds(pl.multiple_of(k * TOK, TOK), TOK)
            total = pacc[rows, :]
            for f in blocks:
                term = tbuf[f, rows, :].astype(jnp.float32) * rowf[f, pl.ds(k, 1), :]
                total = total + (term[:, :128] + term[:, 128:])
            pacc[rows, :] = total

    def half(k):
        return pl.ds(k * (ROWS // 2), ROWS // 2)

    def send_t(dz, k, f=None):
        f = m if f is None else f
        source = tbuf.at[f]
        send(("T", dz, k), source.at[half(k)], tbuf.at[f, half(k)], links["z+" if dz > 0 else "z-"])

    def take_t(d, turn):
        for way in (1, -1):
            dz, k = d * way, turn if way > 0 else 1 - turn
            f = plane(-dz)
            copies["T", dz, k].wait_recv()
            if d < 3 or (d == 3 and turn == 0):
                send_t(dz + way, k, f)
            send(("S", dz, k), tbuf.at[f, half(k)], tbuf.at[f, half(k)], links["s"])
            if turn == 1 or (d == 4 and way > 0):
                copies["R", dz].wait_recv()
                if d < 3 or (d == 3 and way > 0):
                    send(("R", dz + way), rbuf.at[f], rbuf.at[f], links["z+" if way > 0 else "z-"])
                send(("Q", dz), rbuf.at[f], rbuf.at[f], links["s"])

    def take_s(d):
        if d == 1:
            copies["S", 0].wait_recv()
            project([m, plane(0, 1)])
        if d < 4:
            for dz in (d, -d):
                for k in range(2):
                    copies["S", dz, k].wait_recv()
            project([plane(-dz, dc) for dz in (d, -d) for dc in (0, 1)])
        else:
            copies["S", 4, 0].wait_recv()
            copies["S", -4, 1].wait_recv()
            project([plane(4), plane(4, 1)])

            @pl.loop(0, MEMB)
            def _(k):
                rows = pl.ds(pl.multiple_of(k * TOK, TOK), TOK)
                proj = 0.3 * jnp.sum(pacc[rows, :], axis=1, keepdims=True)
                for s in range(2):
                    acc[s, rows, :] += proj * colf[s, pl.ds(k, 1), :]

    def take_w(i, j, s):
        copies["W", i, j, s].wait_recv()
        if j == 0:
            if (i, s) == (1, 0):
                send_w("a+", (2, 0), 0)
            if (i, s) == (3, 1):
                send_w("a-", (2, 0), 1)
            send_w("b+", (i, 1), s)
            send_w("b-", (i, 3), s)
        elif (j, s) == (1, 0):
            send_w("b+", (i, 2), 0)
        elif (j, s) == (3, 1):
            send_w("b-", (i, 2), 1)

    def take_c(i, j, part):
        copies["C", i, j, part].wait_recv()
        if j == 0:
            if i == 1:
                send_c("a+", (2, 0), 0, 0, 32)
            if i == 3:
                send_c("a-", (2, 0), 1, 32, 16)
            if i != 2 or part == 1:
                send_c("b+", (i, 1), 0)
                send_c("b-", (i, 3), 0)
        elif j == 1:
            send_c("b+", (i, 2), 0, 0, 16 if i in (0, 2) else 32)
        elif j == 3:
            lo = 16 if i in (0, 2) else 32
            send_c("b-", (i, 2), 1, lo, 48 - lo)

    def gather(f):
        for s in range(2):
            acc[s] += jnp.dot(tbuf[f], wbuf[f, s], preferred_element_type=jnp.float32)

    def place(f):
        fx, fy = lax.rem(f, N), lax.div(f, N)
        i = lax.rem(a + N - (fx * (1 - c) + fy * c), N)
        j = lax.rem(b + N - (fy * (1 - c) + fx * c), N)
        dz = lax.rem(lax.div(f, 2) + NZ - z, NZ)
        return i, j, jnp.minimum(dz, NZ - dz)

    def early(f):
        i, j, _ = place(f)
        return (i == 0) | (j == 0) | ((i != 2) & (j != 2))

    def first(f):
        i, j, _ = place(f)
        return ((i == 0) & (j != 2)) | (j == 0)

    def gather_first(start):
        @pl.loop(start, start + 2)
        def _(f):
            @pl.when(first(f) & (place(f)[2] <= 2))
            def _():
                gather(f)

    def gather_next(start):
        @pl.loop(start, start + 2)
        def _(f):
            @pl.when(early(f) & jnp.logical_not(first(f)) & (place(f)[2] <= 2))
            def _():
                gather(f)

    def gather_far(dz):
        @pl.loop(0, 2)
        def _(dc):
            f = plane(dz, dc)

            @pl.when(early(f))
            def _():
                gather(f)

    def start_z():
        @pl.when(c == 1)
        def _():
            pl.semaphore_wait(barrier, 5)
            signal(ready.at[1], links["s"])

        @pl.when(c == 0)
        def _():
            pl.semaphore_wait(ready.at[1], 1)

        for turn in range(2):
            send_t(1, turn)
            send_t(-1, 1 - turn)

    def start_r():
        @pl.when(p != m)
        def _():
            pieces(far[:1])[0].wait_recv()

        for dz, link in ((1, "z+"), (-1, "z-")):
            send(("R", dz), rbuf.at[m], rbuf.at[m], links[link])
        send(("Q", 0), rbuf.at[m], rbuf.at[m], links["s"])

    def rest_of_own():
        send_w("a+", (1, 0), 1, own_w(1))
        send_w("a-", (3, 0), 0, own_w(0))
        send_w("b+", (0, 1), 1, own_w(1))
        send_w("b-", (0, 3), 0, own_w(0))

    def delta():
        for dz in (0, 1, -1, 2, -2, 3, -3, 4):
            copies["Q", dz].wait_recv()
        diagonal = lax.broadcasted_iota(jnp.int32, (MEMB, 128), 0) == lax.broadcasted_iota(jnp.int32, (MEMB, 128), 1)
        sums = jnp.zeros((1, 128), jnp.float32)
        squares = jnp.zeros((1, 128), jnp.float32)
        for q in range(POP):
            piece = rbuf[q].astype(jnp.float32)
            rfull[q * MEMB:(q + 1) * MEMB, :] = piece[:MEMB]
            tail = piece[MEMB:, :128]
            value = (tail[0:1] + tail[1:2]) + tail[2:3]
            sums += value
            squares += value * value
            column = jnp.sum(jnp.where(diagonal, value, 0.0), axis=1, keepdims=True)
            shp[q] = jnp.broadcast_to(column, (MEMB, 128))
        mean = jnp.sum(sums, axis=1, keepdims=True) / COUNT
        var = jnp.sum(squares, axis=1, keepdims=True) / COUNT - mean * mean
        scale = jnp.sqrt(var + 1e-05)

        @pl.loop(0, POP // 2)
        def _(t):
            out = pl.ds(pl.multiple_of(t * 48, 48), 48)
            two = (2 * t, 2 * t + 1)
            for h in range(2):
                part = slice(h * MEMB, (h + 1) * MEMB)
                scaled[h, out, :] = jnp.concatenate(
                    [(shp[q][:, 0:1] - mean) / scale * cbuf[q].astype(jnp.float32)[part] / math.sqrt(COUNT) for q in two],
                    axis=0,
                ).astype(jnp.bfloat16)
        left = jnp.transpose(rfull[...]).astype(jnp.bfloat16)
        for h in range(2):
            part = slice(h * HALF, (h + 1) * HALF)
            d = jnp.dot(left, scaled[h], preferred_element_type=jnp.float32)
            neww[:, part] = (wbuf[p, h].astype(jnp.float32) + 0.5 * d).astype(jnp.bfloat16)

    sent = []

    def flush(keep):
        for copy in list(copies.values())[len(sent):len(copies) - keep]:
            copy.wait_send()
            sent.append(copy)

    steps = {
        "W": take_w, "C": take_c, "T": take_t, "I": rest_of_own, "Z": start_z, "R": start_r,
        "A": gather_first, "B": gather_next, "K": gather_far, "G": lambda i, j: gather(src[i, j]), "D": delta, "F": flush, "S": take_s,
    }
    for step in ORDER:
        steps[step[0]](*step[1:])
    flush(12)

    @pl.when(p == m)
    def _():
        for copy in pieces():
            copy.wait_send()

    for s in (1, 0):
        copies["W", 2, 2, s].wait_recv()

        f = src[2, 2]
        h = (acc[s] + jnp.dot(tbuf[f], wbuf[f, s], preferred_element_type=jnp.float32)) / math.sqrt(D)
        keys[:, s * HALF:(s + 1) * HALF] = (jnp.maximum(h, 0.0) ** 2).astype(jnp.bfloat16)

    flush(0)


def local(tokens, weight, fitness, row_factors, col_factors):
    hbm = pl.BlockSpec(memory_space=pl.ANY)
    vmem = pl.BlockSpec(memory_space=pltpu.VMEM)
    bf, f32 = jnp.bfloat16, jnp.float32
    return pl.pallas_call(
        kernel,
        out_shape=(pltpu.VMEM((ROWS, HID), bf), pltpu.VMEM((FEAT, HID), bf)),
        in_specs=[hbm, hbm, pl.BlockSpec(memory_space=pltpu.SMEM), hbm, hbm],
        out_specs=(vmem, vmem),
        scratch_shapes=[
            pltpu.VMEM((MEMB, D), bf),
            pltpu.VMEM((MEMB, HID), bf),
            pltpu.VMEM((POP, 2, FEAT, HALF), bf),
            pltpu.VMEM((2 * NZ, ROWS, FEAT), bf),
            pltpu.VMEM((POP, 2 * MEMB, HALF), bf),
            pltpu.VMEM((POP, 32, FEAT), bf),
            pltpu.VMEM((POP, 32, FEAT), bf),
            pltpu.VMEM((2 * MEMB, HALF), bf),
            pltpu.VMEM((POP, MEMB, FEAT), f32),
            pltpu.VMEM((2, MEMB, HALF), f32),
            pltpu.VMEM((POP, MEMB, 128), f32),
            pltpu.VMEM((2, COUNT, HALF), bf),
            pltpu.VMEM((COUNT, FEAT), f32),
            pltpu.VMEM((2, ROWS, HALF), f32),
            pltpu.VMEM((ROWS, 128), f32),
            pltpu.SemaphoreType.DMA((135,)),
            pltpu.SemaphoreType.DMA((121,)),
            pltpu.SemaphoreType.DMA((5,)),
            pltpu.SemaphoreType.REGULAR((2,)),
        ],
        compiler_params=pltpu.CompilerParams(
            collective_id=0, has_side_effects=True, vmem_limit_bytes=57 << 20
        ),
        cost_estimate=pl.CostEstimate(flops=6_700_000_000, bytes_accessed=4_000_000, transcendentals=0),
    )(tokens, weight, fitness, row_factors, col_factors)


def solution(mesh):
    placed = (P("pop", "mp"), P("pop", "mp"), P("pop"), P("pop", None), P("pop", "mp"))
    return jax.shard_map(
        local,
        mesh=mesh,
        in_specs=placed,
        out_specs=(P("pop", "mp"), P("pop", "mp")),
        check_vma=False,
    )
```
